128 devices in a mesh: gx: 4 (over z_hi, core), gy: 8 (over y, z_lo), gz: 4 (over x).
Axes of the slice: x: 4, y: 4, z: 4 (z_hi: 2, z_lo: 2; z = z_hi * 2 + z_lo), core: 2. Of those that a mesh axis runs over, the one named last changes fastest.
Arguments:
- positions: float32 [8, 16, 8, 3, 128], P('gx', 'gy', 'gz'), may hold values from 0 to 128, as said below
- velocities: float32 [8, 16, 8, 3, 128], P('gx', 'gy', 'gz'), may hold values from -5 to 5
- species: int32 [8, 16, 8, 128], P('gx', 'gy', 'gz'), may hold values from 0 to 3, as said below
- neighbour_blocks: int32 [8, 16, 8, 8], P('gx', 'gy', 'gz'), may hold values from 0 to 27, as said below
- embedding: bfloat16 [4, 64], replicated, may hold values from -6 to 6
- w_send: bfloat16 [2, 64, 64], replicated, may hold values from -0.75 to 0.75
- w_radial: float32 [2, 8, 64], replicated, may hold values from -4 to 4
- w_update: bfloat16 [2, 64, 64], replicated, may hold values from -0.75 to 0.75
- w_out: bfloat16 [64, 64], replicated, may hold values from -0.75 to 0.75
- w_energy: float32 [64], replicated, may hold values from -5 to 5
- masses: float32 [4], replicated, may hold values from 0.5 to 8
Outputs:
- displacement: float32 [8, 16, 8, 3, 128], P('gx', 'gy', 'gz')
- new_velocity: float32 [8, 16, 8, 3, 128], P('gx', 'gy', 'gz')
The draws below stay inside these ranges and needn't reach their ends.
Inputs may be any that keep to these rules, and one draw needn't show every extreme that they name: `positions`: each atom slot lies in the cube of side 8 whose lowest corner is 8 times its block's coordinates. `species`: 0 marks an empty slot; in each block the empty slots follow the occupied ones, and at least 32 slots are occupied. `neighbour_blocks`: entry o below 27 is the offset 9 (dx + 1) + 3 (dy + 1) + (dz + 1) of a source block; 27 marks an empty slot. The first entry is 13, the block itself; live entries of a block are distinct and come before its empty slots; each block has two or more live entries.
All inputs are finite; a program needn't handle non-finite values.
Results may differ from the reference program's by a relative error of at most 0.039.
Values may be sent and summed in bfloat16 or wider, within the bound.
No kernel may reach another device: no remote copies, remote signals or barrier semaphores. Data moves between devices by JAX's collectives and lax.ppermute only.
A program may use at most 64 MiB of HBM per device.

```python
import math
import jax
import jax.numpy as jnp
from jax import lax

C = 64
K = 8
SPECIES = 4
A = 128
NT = 8
STEPS = 1
NBX = 8
NBY = 16
NBZ = 8


block_side = 8.0


def draw_positions(key, part):
    full_shape = (NBX, NBY, NBZ, 3, A)
    component = lax.broadcasted_iota(jnp.int32, full_shape, 3)
    index_x = lax.broadcasted_iota(jnp.float32, full_shape, 0)
    index_y = lax.broadcasted_iota(jnp.float32, full_shape, 1)
    index_z = lax.broadcasted_iota(jnp.float32, full_shape, 2)
    anchor = jnp.where(component == 0, index_x, jnp.where(component == 1, index_y, index_z)) * block_side
    unit_draw = jax.random.uniform(jax.random.fold_in(key, 11), full_shape, jnp.float32)
    return anchor + block_side * unit_draw


def draw_velocities(key, part):
    full_shape = (NBX, NBY, NBZ, 3, A)
    frac_x = lax.broadcasted_iota(jnp.float32, full_shape, 0) / (NBX - 1)
    frac_y = lax.broadcasted_iota(jnp.float32, full_shape, 1) / (NBY - 1)
    frac_z = lax.broadcasted_iota(jnp.float32, full_shape, 2) / (NBZ - 1)
    spread = 0.15 * jnp.exp(0.5 * jnp.log(3.0) * (frac_x + frac_y + frac_z))
    base = jnp.clip(jax.random.normal(jax.random.fold_in(key, 42), full_shape, jnp.float32), -6.0, 6.0)
    return base * spread


def draw_species(key, part):
    key_fill = jax.random.fold_in(key, 21)
    key_kind = jax.random.fold_in(key, 22)
    filled = jax.random.randint(key_fill, (NBX, NBY, NBZ, 1), A // 4, A + 1)
    species_draw = jax.random.randint(key_kind, (NBX, NBY, NBZ, A), 1, SPECIES)
    slot_index = lax.broadcasted_iota(jnp.int32, (NBX, NBY, NBZ, A), 3)
    return jnp.where(slot_index < filled, species_draw, 0).astype(jnp.int32)


def draw_neighbour_blocks(key, part):
    key_rank = jax.random.fold_in(key, 31)
    key_count = jax.random.fold_in(key, 32)
    scores = jax.random.randint(key_rank, (NBX, NBY, NBZ, 26), 0, 1 << 20) * 32
    scores = scores + lax.broadcasted_iota(jnp.int32, (NBX, NBY, NBZ, 26), 3)
    ranking = jnp.argsort(scores, axis=-1, stable=True).astype(jnp.int32)
    others = ranking + (ranking >= 13).astype(jnp.int32)
    listing = jnp.concatenate([jnp.full((NBX, NBY, NBZ, 1), 13, jnp.int32), others[..., :NT - 1]], axis=-1)
    live_count = jax.random.randint(key_count, (NBX, NBY, NBZ, 1), 2, NT + 1)
    slot_index = lax.broadcasted_iota(jnp.int32, (NBX, NBY, NBZ, NT), 3)
    return jnp.where(slot_index < live_count, listing, 27).astype(jnp.int32)


def bell_draw(stream_key, extent, width, reach, kind=jnp.bfloat16):
    return jnp.clip(width * jax.random.normal(stream_key, extent, jnp.float32), -reach, reach).astype(kind)


def setup_inputs(seed: int = 0) -> dict:
    splits = jax.random.split(jax.random.key(seed), 12)
    positions = draw_positions(jax.random.fold_in(splits[11], 71), 0)
    velocities = draw_velocities(jax.random.fold_in(splits[11], 71), 0)
    species = draw_species(jax.random.fold_in(splits[11], 71), 0)
    neighbour_blocks = draw_neighbour_blocks(jax.random.fold_in(splits[11], 71), 0)
    embedding = bell_draw(splits[4], (SPECIES, C), 1.0, 6.0)
    w_send = bell_draw(splits[5], (2, C, C), C ** -0.5, 0.75)
    w_radial = bell_draw(splits[6], (2, K, C), 0.3, 4.0, jnp.float32)
    w_update = bell_draw(splits[7], (2, C, C), C ** -0.5, 0.75)
    w_out = bell_draw(splits[8], (C, C), C ** -0.5, 0.75)
    w_energy = bell_draw(splits[9], (C,), 0.35, 5.0, jnp.float32)
    masses = jnp.clip(jnp.exp(jax.random.uniform(splits[10], (SPECIES,), jnp.float32, math.log(0.5), math.log(8.0))), 0.5, 8.0)
    return {"positions": positions, "velocities": velocities, "species": species, "neighbour_blocks": neighbour_blocks, "embedding": embedding, "w_send": w_send, "w_radial": w_radial, "w_update": w_update, "w_out": w_out, "w_energy": w_energy, "masses": masses}


soft_sq = 0.25
cut_sq = 25.0
gamma_width = 2.56
time_step = 1.0
target_slot = 0.25
tiny_eps = 1e-06

def slot_tables(neighbour_blocks):
    size_x, size_y, size_z, slot_count = neighbour_blocks.shape
    is_live = neighbour_blocks < 27
    offset = jnp.where(is_live, neighbour_blocks, 13)
    step_x = offset // 9 - 1
    step_y = offset // 3 % 3 - 1
    step_z = offset % 3 - 1
    index_x = lax.broadcasted_iota(jnp.int32, neighbour_blocks.shape, 0)
    index_y = lax.broadcasted_iota(jnp.int32, neighbour_blocks.shape, 1)
    index_z = lax.broadcasted_iota(jnp.int32, neighbour_blocks.shape, 2)
    source = ((index_x + 1 + step_x) * (size_y + 2) + (index_y + 1 + step_y)) * (size_z + 2) + (index_z + 1 + step_z)
    target = ((index_x[..., 0] + 1) * (size_y + 2) + index_y[..., 0] + 1) * (size_z + 2) + index_z[..., 0] + 1
    return (source.reshape(-1, slot_count).astype(jnp.int32), target.reshape(-1).astype(jnp.int32), is_live.astype(jnp.float32).reshape(-1, slot_count), (neighbour_blocks == 13).astype(jnp.float32).reshape(-1, slot_count))

def feature_table(species_ext, embedding):
    kind_count = embedding.shape[0]
    onehot = (species_ext[..., None, :] == lax.broadcasted_iota(jnp.int32, (kind_count, 1), 0)).astype(jnp.float32)
    return jnp.einsum('sc,...sa->...ca', embedding.astype(jnp.float32), onehot)

def inverse_mass(species, masses):
    kind_count = masses.shape[0]
    onehot = (species[..., None, :] == lax.broadcasted_iota(jnp.int32, (kind_count, 1), 0)).astype(jnp.float32)
    return 1.0 / jnp.einsum('s,...sa->...a', masses, onehot)[..., None, :]

def pair_kernel(target_pos, target_real, source_pos, source_real, slot_live, slot_self, basis_count):
    offset = source_pos[:, :, None, :] - target_pos[None, :, :, None]
    squared = lax.optimization_barrier(jnp.sum(offset * offset, axis=1))
    distance = jnp.sqrt(squared + soft_sq)
    cutoff = jnp.square(jax.nn.relu(1.0 - squared / cut_sq))
    atom_count = target_pos.shape[-1]
    diagonal = (lax.broadcasted_iota(jnp.int32, (atom_count, atom_count), 0) == lax.broadcasted_iota(jnp.int32, (atom_count, atom_count), 1)).astype(jnp.float32)
    weight = cutoff * target_real[None, :, None] * source_real[:, None, :] * slot_live[:, None, None]
    weight = weight * (1.0 - slot_self[:, None, None] * diagonal[None])
    centers = (lax.iota(jnp.float32, basis_count) + 0.5) * (5.0 / basis_count)
    radial = jnp.exp(-gamma_width * jnp.square(distance[None] - centers[:, None, None, None]))
    return (weight[None] * radial).astype(jnp.bfloat16)

def block_message(kernel, source_feat, w_send, w_radial):
    sender = jnp.einsum('qcj,cd->qdj', source_feat.astype(jnp.bfloat16).astype(jnp.float32), w_send.astype(jnp.float32)).astype(jnp.bfloat16)
    partial_value = jnp.einsum('kqij,qdj->kdi', kernel.astype(jnp.float32), sender.astype(jnp.float32))
    return lax.optimization_barrier(jnp.sum(partial_value * w_radial[:, :, None], axis=0)).astype(jnp.bfloat16)

def block_update(target_feat, message, w_update):
    update = jnp.einsum('ci,cd->di', message.astype(jnp.float32), w_update.astype(jnp.float32))
    return target_feat + jax.nn.silu(update)

def layer_one(flat_pos, flat_feat, flat_real, tables, w_send, w_radial, w_update):

    def one_block(entry):
        source_idx, target_idx, slot_live, slot_self = entry
        kernel = pair_kernel(flat_pos[target_idx], flat_real[target_idx], jnp.take(flat_pos, source_idx, axis=0), jnp.take(flat_real, source_idx, axis=0), slot_live, slot_self, w_radial.shape[1])
        message = block_message(kernel, jnp.take(flat_feat, source_idx, axis=0), w_send[0], w_radial[0])
        return block_update(flat_feat[target_idx], message, w_update[0])
    layer_out = lax.map(jax.checkpoint(one_block), tables)
    return lax.optimization_barrier(layer_out.astype(jnp.bfloat16)).astype(jnp.float32)

def layer_two_energy(flat_pos, flat_feat, flat_real, tables, w_send, w_radial, w_update, w_out, w_energy):

    def one_block(entry):
        source_idx, target_idx, slot_live, slot_self = entry
        target_real = flat_real[target_idx]
        kernel = pair_kernel(flat_pos[target_idx], target_real, jnp.take(flat_pos, source_idx, axis=0), jnp.take(flat_real, source_idx, axis=0), slot_live, slot_self, w_radial.shape[1])
        message = block_message(kernel, jnp.take(flat_feat, source_idx, axis=0), w_send[1], w_radial[1])
        second = block_update(flat_feat[target_idx], message, w_update[1])
        hidden = jnp.einsum('ci,cd->di', second.astype(jnp.bfloat16).astype(jnp.float32), w_out.astype(jnp.float32))
        per_atom = lax.optimization_barrier(jnp.sum(jax.nn.silu(hidden) * w_energy[:, None], axis=0)) * target_real
        return jnp.sum(per_atom)
    return jnp.sum(lax.map(jax.checkpoint(one_block), tables))

def reference(positions, velocities, species, neighbour_blocks, embedding, w_send, w_radial, w_update, w_out, w_energy, masses):
    grid_x, grid_y, grid_z = (positions.shape[0], positions.shape[1], positions.shape[2])
    atom_count = positions.shape[-1]
    channels = w_send.shape[-1]
    species_ext = jnp.pad(species, ((1, 1), (1, 1), (1, 1), (0, 0)))
    flat_feat = feature_table(species_ext, embedding).reshape(-1, channels, atom_count)
    flat_real = (species_ext > 0).astype(jnp.float32).reshape(-1, atom_count)
    tables = slot_tables(neighbour_blocks)
    inverse = inverse_mass(species, masses)
    padding = ((1, 1), (1, 1), (1, 1), (0, 0), (0, 0))

    def total_energy(coords):
        flat_pos = jnp.pad(coords, padding).reshape(-1, 3, atom_count)
        layer_out = layer_one(flat_pos, flat_feat, flat_real, tables, w_send, w_radial, w_update)
        grid_feat = layer_out.reshape(grid_x, grid_y, grid_z, channels, atom_count)
        flat_hidden = jnp.pad(grid_feat, padding).reshape(-1, channels, atom_count)
        return layer_two_energy(flat_pos, flat_hidden, flat_real, tables, w_send, w_radial, w_update, w_out, w_energy)

    def forces(coords):
        return -jax.grad(total_energy)(coords)
    coords = positions
    velocity = velocities
    travelled = jnp.zeros_like(positions)
    force_now = forces(coords)
    for stepno in range(STEPS):
        half_kick = velocity + 0.5 * time_step * force_now * inverse
        coords = coords + time_step * half_kick
        travelled = travelled + time_step * half_kick
        force_now = forces(coords)
        velocity = half_kick + 0.5 * time_step * force_now * inverse
    real_here = (species > 0).astype(jnp.float32)[..., None, :]
    kinetic = jnp.sum(real_here * 0.5 / inverse * velocity * velocity)
    slot_total = positions.size // 3
    factor = jnp.sqrt(target_slot * slot_total / (kinetic + tiny_eps))
    return (travelled, velocity * factor)
```

```python
import math

import jax
import jax.numpy as jnp
from jax import lax
from jax.experimental import pallas as pl
from jax.experimental.pallas import tpu as pltpu
from jax.sharding import PartitionSpec as P

AXES = ("gx", "gy", "gz")
FAR = 1e12
FAR_TEST = 1e11
HUGE = 1e30
LOG2E = 1.4426950408889634
A = 128
C = 64
K = 8
NB = 8
NE = 64
ROWS = 32
PAY = 80
BF = jnp.bfloat16
F32 = jnp.float32
time_step = 1.0
target_slot = 0.25
tiny_eps = 1e-06


def ring(cells, axis, sign):
    count = lax.axis_size(axis)
    return lax.ppermute(cells, axis, [(i, (i + sign) % count) for i in range(count)])


def halo_up(cells):
    for dim, axis in enumerate(AXES):
        cells = jnp.concatenate([cells, ring(cells, axis, -1)], axis=dim)
    return cells


def halo_down(cells):
    for dim, axis in enumerate(AXES):
        cells = jnp.concatenate([ring(cells, axis, 1), cells], axis=dim)
    return cells


def fold_down(grid, kind):
    for dim in (2, 1, 0):
        low = lax.slice_in_dim(grid, 0, 2, axis=dim).astype(kind)
        grid = lax.slice_in_dim(grid, 2, 4, axis=dim) + ring(low, AXES[dim], -1).astype(F32)
    return grid


def fold_up(grid):
    for dim in (2, 1, 0):
        high = lax.slice_in_dim(grid, 2, 4, axis=dim)
        grid = lax.slice_in_dim(grid, 0, 2, axis=dim) + ring(high, AXES[dim], 1)
    return grid


def slot_sources(lists, shift):
    live = lists < 27
    offset = jnp.where(live, lists, 13)
    steps = (offset // 9 - 1, offset // 3 % 3 - 1, offset % 3 - 1)
    source = jnp.zeros_like(lists)
    for dim, axis in enumerate(AXES):
        total = 2 * lax.axis_size(axis)
        place = lax.broadcasted_iota(jnp.int32, lists.shape, dim)
        here = (2 * lax.axis_index(axis) + shift + place) % total + steps[dim]
        live = live & (here >= 0) & (here < total)
        source = source * 4 + place + 1 + steps[dim]
    return jnp.where(live, source, -1).reshape(NB, 8)


def dot(a, b):
    return lax.dot_general(a, b, (((1,), (0,)), ((), ())), preferred_element_type=F32)


def dot_nt(a, b):
    return lax.dot_general(a, b, (((1,), (1,)), ((), ())), preferred_element_type=F32)


def silu_grad(x):
    gate = jax.nn.sigmoid(x)
    return gate * (1.0 + x * (1.0 - gate))


def target_index(b):
    return ((b // 4 + 1) * 4 + (b // 2 % 2 + 1)) * 4 + b % 2 + 1


DEAD = 1024


def live_pairs(src_ref, pairs):
    count = jnp.int32(1)
    pairs[0] = DEAD
    for b in range(NB):
        for q in range(8):
            entry = src_ref[b, q]
            pairs[count] = entry + NE * b + jnp.where(entry == target_index(b), 0, 512)
            count = count + (entry >= 0).astype(jnp.int32)
    pairs[count] = DEAD
    pairs[count + 1] = DEAD
    return count - 1


def decode(code):
    return code % NE, code // NE % NB, code // 512


def fill_diag(diag):
    rows = lax.broadcasted_iota(jnp.int32, (A, A), 0)
    cols = lax.broadcasted_iota(jnp.int32, (A, A), 1)
    diag[0:A, :] = jnp.where(rows == cols, HUGE, 0.0)
    diag[A : 2 * A, :] = jnp.zeros((A, A), F32)
    diag[2 * A : 3 * A, :] = jnp.full((A, A), HUGE, F32)


def at(start, size):
    return pl.ds(pl.multiple_of(start, size), size)


def pair_squared(pcol, diag, src, kind, r, rows):
    cols = pcol[at(src * A + r, ROWS), :]
    dx = cols[:, 0:1] - rows[0:1, :]
    dy = cols[:, 1:2] - rows[1:2, :]
    dz = cols[:, 2:3] - rows[2:3, :]
    return jnp.minimum(dx * dx + dy * dy + dz * dz + diag[at(kind * A + r, ROWS), :], 25.0)


def pair_terms(squared):
    soft = squared + 0.25
    inv = lax.rsqrt(soft)
    u = soft * inv * 1.6 - 0.5
    t = 1.0 - squared * 0.04
    bell = jnp.exp2(u * u * (-LOG2E))
    growth = jnp.exp2(u * (2.0 * LOG2E))
    return inv, u, t, bell, growth


def store_kernel(pcol, diag, kern, sq, base, src, kind, rows):
    for r in range(0, A, ROWS):
        squared = pair_squared(pcol, diag, src, kind, r, rows)
        if sq is not None:
            sq[at(base + r, ROWS), :] = squared
        _, _, t, bell, growth = pair_terms(squared)
        value = bell * t * t
        for k in range(K):
            kern[at(base + r, ROWS), k * A : (k + 1) * A] = (value * math.exp(-k * k)).astype(BF)
            if k < K - 1:
                value = value * growth


def pair_slopes(squared_of, dker, slope):
    for r in range(0, A, ROWS):
        inv, u, t, bell, growth = pair_terms(squared_of(r))
        def weight(k):
            return dker[r : r + ROWS, tile(k)].astype(F32) * math.exp(-k * k)

        value = weight(K - 1)
        first = value
        for k in range(K - 2, 0, -1):
            value = value * growth + weight(k)
            first = first * growth + value
        first = first * growth
        value = value * growth + weight(0)
        out = (bell * t) * (value * (-0.08) + (t * inv * 1.6) * (first - u * value))
        high, low = halves(out)
        slope[r : r + ROWS, :] = high
        slope[A + r : A + r + ROWS, :] = low


def split16(rel):
    high = rel.astype(BF).astype(F32)
    return jnp.concatenate([high, rel - high], axis=0).astype(BF)


def halves(value):
    high = value.astype(BF)
    return high, (value - high.astype(F32)).astype(BF)


def dot_wide(weights, value):
    high, low = halves(value)
    return dot(weights, high) + dot(weights, low)


def moment_grad(rel, moments):
    total = moments[0:8, :] + moments[8:16, :]
    return 2.0 * (rel * total[3:4, :] - total)


def marked(rows):
    place = lax.broadcasted_iota(jnp.int32, (8, A), 0)
    return jnp.where(place == 3, 1.0, jnp.where(place < 3, rows, 0.0))


def species_onehot(row):
    return (lax.broadcasted_iota(jnp.int32, (8, A), 0).astype(F32) == row).astype(BF)


def reference_point(rows):
    place = lax.broadcasted_iota(jnp.int32, (8, A), 0)
    return jnp.where(place < 3, rows[:, 0:1], 0.0)


def tile(b):
    return slice(b * A, (b + 1) * A)


def forward_pairs(count, pairs, pcol, diag, kern, sq, acc, lhs, rows_of, slots):
    kern[0:A, :] = jnp.zeros((A, K * A), BF)
    acc[...] = jnp.zeros_like(acc)

    def multiply(n):
        src, b, _ = decode(pairs[n])
        acc[b] = acc[b] + dot(lhs[src], kern[at(n % slots * A, A), :])

    def step(n, carry):
        multiply(n - 1)
        src, b, kind = decode(pairs[n])
        store_kernel(pcol, diag, kern, sq, n % slots * A, src, kind, rows_of(target_index(b)))
        return carry

    lax.fori_loop(1, count + 1, step, 0)
    multiply(count)


def backward_pairs(
    count, pairs, p8, squared_of, dkers, slopes, s_rows, gt, pg, relt, splt, refs, tacc, extra
):
    tacc[...] = jnp.zeros_like(tacc)

    def slope_weights(n, dker):
        src, b, _ = decode(pairs[n])
        dker[...] = dot(jnp.concatenate([s_rows[at(src * A, A), :]] * 2, axis=1), gt[b]).astype(BF)

    def moments(n, slope):
        src, b, _ = decode(pairs[n])
        rel_s = p8[src] - refs[b]
        split_s = split16(rel_s)
        side_t = dot(jnp.concatenate([split_s, split_s], axis=1), slope[...])
        side_s = dot_nt(splt[b], slope[0:A, :]) + dot_nt(splt[b], slope[A:, :])
        pg[src] = pg[src] + moment_grad(rel_s, side_s)
        tacc[b] = tacc[b] + moment_grad(relt[b], side_t)

    slope_weights(1, dkers[0])

    def step(m, carry):
        n = 2 * m + 1
        slope_weights(n + 1, dkers[1])
        pair_slopes(squared_of(n), dkers[0], slopes[0])
        extra(n)
        slope_weights(n + 2, dkers[0])
        moments(n, slopes[0])
        pair_slopes(squared_of(n + 1), dkers[1], slopes[1])
        extra(n + 1)
        moments(n + 1, slopes[1])
        return carry

    lax.fori_loop(0, (count + 1) // 2, step, 0)
    for b in range(NB):
        pg[target_index(b)] = pg[target_index(b)] + tacc[b]


def spread_weights(wr, dmsg, gt):
    for b in range(NB):
        for k in range(K):
            high, low = halves(wr[:, k : k + 1] * dmsg[:, tile(b)])
            gt[b, 0:C, tile(k)] = high
            gt[b, C : 2 * C, tile(k)] = low


def place_targets(p8, relt, splt, refs):
    for b in range(NB):
        rows = p8[target_index(b)]
        refs[b] = reference_point(rows)
        relt[b] = rows - refs[b]
        splt[b] = split16(relt[b])


def first_forward(src_ref, xe, embt, wks, wut, pay_ref, upd_ref, pcol, diag, kern, acc, hot, cat, pairs):
    fill_diag(diag)
    count = live_pairs(src_ref, pairs)

    def prepare(n, carry):
        rows = xe[n]
        pcol[at(n * A, A), :] = rows.T
        hot[n] = species_onehot(rows[3:4, :])
        return carry

    lax.fori_loop(0, NE, prepare, 0, unroll=8)
    forward_pairs(count, pairs, pcol, diag, kern, None, acc, hot, lambda i: xe[i], 2)
    for b in range(NB):
        for k in range(K):
            cat[k * 8 : (k + 1) * 8, tile(b)] = acc[b, :, tile(k)]
    w_high, w_low = halves(wks[...])
    c_high, c_low = halves(cat[...])
    msg = dot(w_high, c_high) + (dot(w_high, c_low) + dot(w_low, c_high))
    upd = dot(wut[...], msg.astype(BF))
    upd_ref[...] = upd
    gain = upd * jax.nn.sigmoid(upd)
    for b in range(NB):
        rows = xe[target_index(b)]
        h0 = dot(embt[...], species_onehot(rows[3:4, :]))
        pay_ref[b, 0:C, :] = (h0 + gain[:, tile(b)]).astype(BF)
        pos = marked(rows)
        high = pos.astype(BF).astype(F32)
        mid = (pos - high).astype(BF).astype(F32)
        low = pos - high - mid
        place = lax.broadcasted_iota(jnp.int32, (8, A), 0)
        tail = jnp.where(place < 3, mid, 0.0) + jnp.where(place >= 4, jnp.roll(low, 4, axis=0), 0.0)
        pay_ref[b, C:PAY, :] = jnp.concatenate([high, tail], axis=0).astype(BF)


def second_both(
    src_ref, hx, ws, wst, wr, wu, wut, wo, wot, we, out_ref,
    pcol, p8, diag, kern, sq, acc, st, s_rows, gt, dker0, dker1, slope0, slope1, ds, pg, relt, splt, refs, tacc, wide, pairs,
):
    fill_diag(diag)
    count = live_pairs(src_ref, pairs)

    def prepare(n, carry):
        tail = hx[n, C:PAY, :].astype(F32)
        high, rest = tail[0:8, :], tail[8:16, :]
        place = lax.broadcasted_iota(jnp.int32, (8, A), 0)
        low = jnp.roll(rest, 4, axis=0)
        pos = high + jnp.where(place < 3, rest, 0.0) + jnp.where(place < 3, low, 0.0)
        p8[n] = pos
        pcol[at(n * A, A), :] = pos.T
        sender = dot(wst[...], hx[n, 0:C, :]).astype(BF).astype(F32)
        st[n] = sender.astype(BF)
        s_rows[at(n * A, A), :] = sender.T.astype(BF)
        ds[n] = jnp.zeros((C, A), F32)
        pg[n] = jnp.zeros((8, A), F32)
        return carry

    lax.fori_loop(0, NE, prepare, 0, unroll=8)
    place_targets(p8, relt, splt, refs)
    forward_pairs(count, pairs, pcol, diag, kern, sq, acc, st, lambda i: p8[i], NE + 2)
    kern[at((count + 1) * A, A), :] = jnp.zeros((A, K * A), BF)
    sq[at((count + 1) * A, A), :] = jnp.full((A, A), 25.0, F32)
    for b in range(NB):
        total = wr[:, 0:1] * acc[b, :, tile(0)]
        for k in range(1, K):
            total = total + wr[:, k : k + 1] * acc[b, :, tile(k)]
        wide[:, tile(b)] = total
    upd = dot(wut[...], wide[...].astype(BF))
    gain = upd * jax.nn.sigmoid(upd)
    for b in range(NB):
        wide[:, tile(b)] = hx[target_index(b), 0:C, :].astype(F32) + gain[:, tile(b)]
    hidden = dot(wot[...], wide[...].astype(BF))
    dhid = silu_grad(hidden) * we[:, 0:1]
    for b in range(NB):
        real = (p8[target_index(b), 0:1, :] < FAR_TEST).astype(F32)
        wide[:, tile(b)] = dhid[:, tile(b)] * real
    dh2 = dot_wide(wo[...], wide[...]).astype(BF).astype(F32)
    dmsg = dot_wide(wu[...], dh2 * silu_grad(upd)).astype(BF).astype(F32)
    spread_weights(wr, dmsg, gt)
    wide[...] = dh2

    def senders(n):
        src, b, _ = decode(pairs[n])
        both = dot_nt(gt[b], kern[at(n * A, A), :])
        back = dot(ws[...], (both[0:C] + both[C:]).astype(BF))
        ds[src] = ds[src] + back.astype(BF).astype(F32)

    def squared_of(n):
        return lambda r: sq[at(n * A + r, ROWS), :]

    backward_pairs(
        count, pairs, p8, squared_of, (dker0, dker1), (slope0, slope1), s_rows, gt, pg, relt, splt, refs, tacc, senders
    )

    def finish(n, carry):
        out_ref[n, 0:C, :] = ds[n]
        out_ref[n, C : C + 8, :] = pg[n]
        return carry

    lax.fori_loop(0, NE, finish, 0, unroll=8)
    for b in range(NB):
        out_ref[target_index(b), 0:C, :] = out_ref[target_index(b), 0:C, :] + wide[:, tile(b)]


def first_backward(
    src_ref, xe, dh, upd_ref, embt, wst, wr, wu, pg,
    pcol, p8, diag, s_rows, gt, dker0, dker1, slope0, slope1, relt, splt, refs, tacc, wide, pairs,
):
    fill_diag(diag)
    count = live_pairs(src_ref, pairs)
    table = dot(wst[...], embt[...]).astype(BF)

    def prepare(n, carry):
        rows = xe[n]
        pcol[at(n * A, A), :] = rows.T
        p8[n] = marked(rows)
        sender = dot(table, species_onehot(rows[3:4, :]))
        s_rows[at(n * A, A), :] = sender.T.astype(BF)
        pg[n] = jnp.zeros((8, A), F32)
        return carry

    lax.fori_loop(0, NE, prepare, 0, unroll=8)
    place_targets(p8, relt, splt, refs)
    for b in range(NB):
        real = (p8[target_index(b), 0:1, :] < FAR_TEST).astype(F32)
        wide[:, tile(b)] = dh[b, 0:C, :].astype(BF).astype(F32) * real
    dmsg = dot_wide(wu[...], wide[...] * silu_grad(upd_ref[...])).astype(BF).astype(F32)
    spread_weights(wr, dmsg, gt)

    def squared_of(n):
        src, b, kind = decode(pairs[n])
        rows = p8[target_index(b)]
        return lambda r: pair_squared(pcol, diag, src, kind, r, rows)

    backward_pairs(
        count, pairs, p8, squared_of, (dker0, dker1), (slope0, slope1), s_rows, gt, pg, relt, splt, refs, tacc,
        lambda n: None,
    )
    for b in range(NB):
        pg[target_index(b)] = pg[target_index(b)] + dh[b, C : C + 8, :]


SM = pl.BlockSpec(memory_space=pltpu.SMEM)
VM = pl.BlockSpec(memory_space=pltpu.VMEM)


def vm(*shape, kind=F32):
    return pltpu.VMEM(shape, kind)


PAIRS = pltpu.SMEM((NE + 4,), jnp.int32)


def params(mib):
    return pltpu.CompilerParams(vmem_limit_bytes=mib * 2**20)


def backward_scratch():
    return [vm(NB, 8, A), vm(NB, 16, A, kind=BF), vm(NB, 8, A), vm(NB, 8, A), vm(C, NB * A), PAIRS]


def call_first_forward(src, xe, *weights):
    return pl.pallas_call(
        first_forward,
        out_shape=(jax.ShapeDtypeStruct((NB, PAY, A), BF), jax.ShapeDtypeStruct((C, NB * A), F32)),
        in_specs=[SM] + [VM] * (1 + len(weights)),
        out_specs=(VM, VM),
        scratch_shapes=[
            vm(NE * A, 8), vm(3 * A, A), vm(2 * A, K * A, kind=BF), vm(NB, 8, K * A), vm(NE, 8, A, kind=BF),
            vm(C, NB * A), PAIRS,
        ],
        compiler_params=params(20),
        name="first_forward",
    )(src, xe, *weights)


def call_second(src, hx, *weights):
    return pl.pallas_call(
        second_both,
        out_shape=jax.ShapeDtypeStruct((NE, C + 8, A), F32),
        in_specs=[SM] + [VM] * (1 + len(weights)),
        out_specs=VM,
        scratch_shapes=[
            vm(NE * A, 8), vm(NE, 8, A), vm(3 * A, A), vm((NE + 2) * A, K * A, kind=BF), vm((NE + 2) * A, A),
            vm(NB, C, K * A), vm(NE, C, A, kind=BF), vm(NE * A, C, kind=BF), vm(NB, 2 * C, K * A, kind=BF),
            vm(A, K * A, kind=BF), vm(A, K * A, kind=BF), vm(2 * A, A, kind=BF), vm(2 * A, A, kind=BF), vm(NE, C, A), vm(NE, 8, A),
        ] + backward_scratch(),
        compiler_params=params(54),
        name="second_both",
    )(src, hx, *weights)


def call_first_backward(src, xe, dh, upd, *weights):
    return pl.pallas_call(
        first_backward,
        out_shape=jax.ShapeDtypeStruct((NE, 8, A), F32),
        in_specs=[SM] + [VM] * (3 + len(weights)),
        out_specs=VM,
        scratch_shapes=[
            vm(NE * A, 8), vm(NE, 8, A), vm(3 * A, A), vm(NE * A, C, kind=BF), vm(NB, 2 * C, K * A, kind=BF),
            vm(A, K * A, kind=BF), vm(A, K * A, kind=BF), vm(2 * A, A, kind=BF), vm(2 * A, A, kind=BF),
        ] + backward_scratch(),
        compiler_params=params(24),
        name="first_backward",
    )(src, xe, dh, upd, *weights)


def total_over_devices(value):
    count = lax.axis_size(AXES[0]) * lax.axis_size(AXES[1]) * lax.axis_size(AXES[2])
    rows = lax.all_to_all(jnp.broadcast_to(value, (count, 128)), AXES, 0, 0)
    return jnp.sum(rows[:, 0])


def local(
    positions, velocities, species, neighbour_blocks, embedding, w_send, w_radial, w_update, w_out, w_energy, masses
):
    kinds = embedding.shape[0]
    real = (species > 0)[..., None, :]
    inverse = 1.0 / masses[0]
    for s in range(1, kinds):
        inverse = jnp.where(species == s, 1.0 / masses[s], inverse)
    inverse = inverse[..., None, :]

    embt = jnp.pad(embedding.T, ((0, 0), (0, 8 - kinds)))
    wr = jnp.swapaxes(w_radial, 1, 2)
    wst = jnp.swapaxes(w_send, 1, 2)
    wut = jnp.swapaxes(w_update, 1, 2)
    we = w_energy[:, None]
    table = lax.reduce_precision(dot(wst[0], embt), 8, 7)
    wks = (wr[0][:, :, None] * table[:, None, :]).reshape(C, K * 8)

    lists = jnp.pad(neighbour_blocks.astype(F32), ((0, 0),) * 3 + ((0, A - 8),))[..., None, :]
    rest = jnp.concatenate(
        [species.astype(F32)[..., None, :], lists, jnp.zeros(species.shape[:3] + (3, A), F32)], axis=3
    )
    component = lax.broadcasted_iota(jnp.int32, positions.shape, 3)

    def placed(coords):
        away = jnp.where(real | (component > 0), coords, FAR)
        return halo_up(jnp.concatenate([away, rest], axis=3))

    own_src = slot_sources(neighbour_blocks, 0)

    def forces(ext, up_src):
        xe = ext.reshape(NE, 8, A)
        pay, upd = call_first_forward(up_src, xe, embt, wks, wut[0])
        hx = halo_down(pay.reshape(2, 2, 2, PAY, A)).reshape(NE, PAY, A)
        grads = call_second(
            own_src, hx, w_send[1], wst[1], wr[1], w_update[1], wut[1], w_out, w_out.T, we
        )
        folded = fold_down(grads.reshape(4, 4, 4, C + 8, A), BF).reshape(NB, C + 8, A)
        slopes = call_first_backward(up_src, xe, folded, upd, embt, wst[0], wr[0], w_update[0])
        return -fold_up(slopes.reshape(4, 4, 4, 8, A))[:, :, :, 0:3, :]

    ext = placed(positions)
    up_src = slot_sources(
        ext[1:3, 1:3, 1:3, 4, 0:8].astype(jnp.int32), 1
    )
    force_now = forces(ext, up_src)
    half_kick = velocities + 0.5 * time_step * force_now * inverse
    coords = positions + time_step * half_kick
    travelled = time_step * half_kick
    force_now = forces(placed(coords), up_src)
    velocity = half_kick + 0.5 * time_step * force_now * inverse
    local_kinetic = jnp.sum(real.astype(F32) * 0.5 / inverse * velocity * velocity)
    kinetic = total_over_devices(local_kinetic)
    slot_total = positions.size // 3 * lax.axis_size("gx") * lax.axis_size("gy") * lax.axis_size("gz")
    factor = jnp.sqrt(target_slot * slot_total / (kinetic + tiny_eps))
    return (travelled, velocity * factor)


def solution(mesh):
    spatial5 = P("gx", "gy", "gz", None, None)
    spatial4 = P("gx", "gy", "gz", None)
    return jax.shard_map(
        local,
        mesh=mesh,
        in_specs=(spatial5, spatial5, spatial4, spatial4) + (P(),) * 7,
        out_specs=(spatial5, spatial5),
        check_vma=False,
    )
```

```python
import math

import jax
import jax.numpy as jnp
from jax import lax
from jax.experimental import pallas as pl
from jax.experimental.pallas import tpu as pltpu
from jax.sharding import PartitionSpec as P

AXES = ("gx", "gy", "gz")
FAR = 1e12
FAR_TEST = 1e11
HUGE = 1e30
LOG2E = 1.4426950408889634
A = 128
C = 64
K = 8
NB = 8
NE = 64
ROWS = 32
HALF = 32
BF = jnp.bfloat16
F32 = jnp.float32
time_step = 1.0
target_slot = 0.25
tiny_eps = 1e-06


def ring(cells, axis, sign):
    count = lax.axis_size(axis)
    return lax.ppermute(cells, axis, [(i, (i + sign) % count) for i in range(count)])


def halo_up(cells):
    for dim, axis in enumerate(AXES):
        cells = jnp.concatenate([cells, ring(cells, axis, -1)], axis=dim)
    return cells


def halo_down(cells, order):
    for dim in order:
        cells = jnp.concatenate([ring(cells, AXES[dim], 1), cells], axis=dim)
    return cells


def fold_down(grid, order):
    for dim in order:
        low = lax.slice_in_dim(grid, 0, 2, axis=dim).astype(BF)
        grid = lax.slice_in_dim(grid, 2, 4, axis=dim) + ring(low, AXES[dim], -1).astype(F32)
    return grid


def fold_up(grid):
    for dim in (2, 1, 0):
        high = lax.slice_in_dim(grid, 2, 4, axis=dim)
        grid = lax.slice_in_dim(grid, 0, 2, axis=dim) + ring(high, AXES[dim], 1)
    return grid


def slot_sources(lists, shift):
    live = lists < 27
    offset = jnp.where(live, lists, 13)
    steps = (offset // 9 - 1, offset // 3 % 3 - 1, offset % 3 - 1)
    source = jnp.zeros_like(lists)
    for dim, axis in enumerate(AXES):
        total = 2 * lax.axis_size(axis)
        place = lax.broadcasted_iota(jnp.int32, lists.shape, dim)
        here = (2 * lax.axis_index(axis) + shift + place) % total + steps[dim]
        live = live & (here >= 0) & (here < total)
        source = source * 4 + place + 1 + steps[dim]
    return jnp.where(live, source, -1).reshape(NB, 8)


def dot(a, b):
    return lax.dot_general(a, b, (((1,), (0,)), ((), ())), preferred_element_type=F32)


def dot_nt(a, b):
    return lax.dot_general(a, b, (((1,), (1,)), ((), ())), preferred_element_type=F32)


def silu_grad(x):
    gate = jax.nn.sigmoid(x)
    return gate * (1.0 + x * (1.0 - gate))


def target_index(b):
    return ((b // 4 + 1) * 4 + (b // 2 % 2 + 1)) * 4 + b % 2 + 1


DEAD = 1024


def live_pairs(src_ref, pairs):
    count = jnp.int32(1)
    pairs[0] = DEAD
    for b in range(NB):
        for q in range(8):
            entry = src_ref[b, q]
            pairs[count] = entry + NE * b + jnp.where(entry == target_index(b), 0, 512)
            count = count + (entry >= 0).astype(jnp.int32)
    pairs[count] = DEAD
    pairs[count + 1] = DEAD
    return count - 1


def decode(code):
    return code % NE, code // NE % NB, code // 512


def fill_diag(diag):
    rows = lax.broadcasted_iota(jnp.int32, (A, A), 0)
    cols = lax.broadcasted_iota(jnp.int32, (A, A), 1)
    diag[0:A, :] = jnp.where(rows == cols, HUGE, 0.0)
    diag[A : 2 * A, :] = jnp.zeros((A, A), F32)
    diag[2 * A : 3 * A, :] = jnp.full((A, A), HUGE, F32)


def at(start, size):
    return pl.ds(pl.multiple_of(start, size), size)


def pair_squared(pcol, diag, src, kind, r, rows):
    cols = pcol[at(src * A + r, ROWS), :]
    dx = cols[:, 0:1] - rows[0:1, :]
    dy = cols[:, 1:2] - rows[1:2, :]
    dz = cols[:, 2:3] - rows[2:3, :]
    return jnp.minimum(dx * dx + dy * dy + dz * dz + diag[at(kind * A + r, ROWS), :], 25.0)


def pair_terms(squared):
    soft = squared + 0.25
    inv = lax.rsqrt(soft)
    u = soft * inv * 1.6 - 0.5
    t = 1.0 - squared * 0.04
    bell = jnp.exp2(u * u * (-LOG2E))
    growth = jnp.exp2(u * (2.0 * LOG2E))
    return inv, u, t, bell, growth


def store_kernel(pcol, diag, kern, sq, base, src, kind, rows):
    for r in range(0, A, ROWS):
        squared = pair_squared(pcol, diag, src, kind, r, rows)
        if sq is not None:
            sq[at(base + r, ROWS), :] = squared
        _, _, t, bell, growth = pair_terms(squared)
        value = bell * t * t
        for k in range(K):
            kern[at(base + r, ROWS), k * A : (k + 1) * A] = (value * math.exp(-k * k)).astype(BF)
            if k < K - 1:
                value = value * growth


def pair_slopes(squared_of, dker, slope):
    for r in range(0, A, ROWS):
        inv, u, t, bell, growth = pair_terms(squared_of(r))
        def weight(k):
            return dker[r : r + ROWS, tile(k)].astype(F32) * math.exp(-k * k)

        value = weight(K - 1)
        first = value
        for k in range(K - 2, 0, -1):
            value = value * growth + weight(k)
            first = first * growth + value
        first = first * growth
        value = value * growth + weight(0)
        out = (bell * t) * (value * (-0.08) + (t * inv * 1.6) * (first - u * value))
        high, low = halves(out)
        slope[r : r + ROWS, :] = high
        slope[A + r : A + r + ROWS, :] = low


def split16(rel):
    high = rel.astype(BF).astype(F32)
    return jnp.concatenate([high, rel - high], axis=0).astype(BF)


def halves(value):
    high = value.astype(BF)
    return high, (value - high.astype(F32)).astype(BF)


def dot_wide(weights, value):
    high, low = halves(value)
    return dot(weights, high) + dot(weights, low)


def moment_grad(rel, moments):
    total = moments[0:8, :] + moments[8:16, :]
    return 2.0 * (rel * total[3:4, :] - total)


def marked(rows):
    place = lax.broadcasted_iota(jnp.int32, (8, A), 0)
    return jnp.where(place == 3, 1.0, jnp.where(place < 3, rows, 0.0))


def species_onehot(row):
    return (lax.broadcasted_iota(jnp.int32, (8, A), 0).astype(F32) == row).astype(BF)


def reference_point(rows):
    place = lax.broadcasted_iota(jnp.int32, (8, A), 0)
    return jnp.where(place < 3, rows[:, 0:1], 0.0)


def tile(b):
    return slice(b * A, (b + 1) * A)


def forward_pairs(count, pairs, pcol, diag, kern, sq, acc, lhs, rows_of, slots):
    kern[0:A, :] = jnp.zeros((A, K * A), BF)
    acc[...] = jnp.zeros_like(acc)

    def multiply(n):
        src, b, _ = decode(pairs[n])
        acc[b] = acc[b] + dot(lhs[src], kern[at(n % slots * A, A), :])

    def step(n, carry):
        multiply(n - 1)
        src, b, kind = decode(pairs[n])
        store_kernel(pcol, diag, kern, sq, n % slots * A, src, kind, rows_of(target_index(b)))
        return carry

    lax.fori_loop(1, count + 1, step, 0)
    multiply(count)


def backward_pairs(
    count, pairs, p8, squared_of, dkers, slopes, s_rows, gt, pg, relt, splt, refs, tacc, extra
):
    tacc[...] = jnp.zeros_like(tacc)

    def slope_weights(n, dker):
        src, b, _ = decode(pairs[n])
        dker[...] = dot(jnp.concatenate([s_rows[at(src * A, A), :]] * 2, axis=1), gt[b]).astype(BF)

    def moments(n, slope):
        src, b, _ = decode(pairs[n])
        rel_s = p8[src] - refs[b]
        split_s = split16(rel_s)
        side_t = dot(jnp.concatenate([split_s, split_s], axis=1), slope[...])
        side_s = dot_nt(splt[b], slope[0:A, :]) + dot_nt(splt[b], slope[A:, :])
        pg[src] = pg[src] + moment_grad(rel_s, side_s)
        tacc[b] = tacc[b] + moment_grad(relt[b], side_t)

    slope_weights(1, dkers[0])

    def step(m, carry):
        n = 2 * m + 1
        slope_weights(n + 1, dkers[1])
        pair_slopes(squared_of(n), dkers[0], slopes[0])
        extra(n)
        slope_weights(n + 2, dkers[0])
        moments(n, slopes[0])
        pair_slopes(squared_of(n + 1), dkers[1], slopes[1])
        extra(n + 1)
        moments(n + 1, slopes[1])
        return carry

    lax.fori_loop(0, (count + 1) // 2, step, 0)
    for b in range(NB):
        pg[target_index(b)] = pg[target_index(b)] + tacc[b]


def spread_weights(wr, dmsg, gt):
    for b in range(NB):
        for k in range(K):
            high, low = halves(wr[:, k : k + 1] * dmsg[:, tile(b)])
            gt[b, 0:C, tile(k)] = high
            gt[b, C : 2 * C, tile(k)] = low


def place_targets(p8, relt, splt, refs):
    for b in range(NB):
        rows = p8[target_index(b)]
        refs[b] = reference_point(rows)
        relt[b] = rows - refs[b]
        splt[b] = split16(relt[b])


def first_forward(src_ref, xe, embt, wks, wut, paya_ref, payb_ref, upd_ref, pcol, diag, kern, acc, hot, cat, pairs):
    fill_diag(diag)
    count = live_pairs(src_ref, pairs)

    def prepare(n, carry):
        rows = xe[n]
        pcol[at(n * A, A), :] = rows.T
        hot[n] = species_onehot(rows[3:4, :])
        return carry

    lax.fori_loop(0, NE, prepare, 0, unroll=8)
    forward_pairs(count, pairs, pcol, diag, kern, None, acc, hot, lambda i: xe[i], 2)
    for b in range(NB):
        for k in range(K):
            cat[k * 8 : (k + 1) * 8, tile(b)] = acc[b, :, tile(k)]
    w_high, w_low = halves(wks[...])
    c_high, c_low = halves(cat[...])
    msg = dot(w_high, c_high) + (dot(w_high, c_low) + dot(w_low, c_high))
    upd = dot(wut[...], msg.astype(BF))
    upd_ref[...] = upd
    gain = upd * jax.nn.sigmoid(upd)
    for b in range(NB):
        rows = xe[target_index(b)]
        h0 = dot(embt[...], species_onehot(rows[3:4, :]))
        h1 = h0 + gain[:, tile(b)]
        paya_ref[b, 0:HALF, :] = h1[0:HALF].astype(BF)
        payb_ref[b] = h1[HALF:].astype(BF)
        pos = marked(rows)
        high = pos.astype(BF).astype(F32)
        mid = (pos - high).astype(BF).astype(F32)
        low = pos - high - mid
        place = lax.broadcasted_iota(jnp.int32, (8, A), 0)
        tail = jnp.where(place < 3, mid, 0.0) + jnp.where(place >= 4, jnp.roll(low, 4, axis=0), 0.0)
        paya_ref[b, HALF:, :] = jnp.concatenate([high, tail], axis=0).astype(BF)


def second_both(
    src_ref, hxa, hxb, ws, wst, wr, wu, wut, wo, wot, we, outa_ref, outb_ref,
    pcol, p8, diag, kern, sq, acc, st, s_rows, gt, dker0, dker1, slope0, slope1, ds, pg, relt, splt, refs, tacc, wide, pairs,
):
    fill_diag(diag)
    count = live_pairs(src_ref, pairs)

    def features(n):
        return jnp.concatenate([hxa[n, 0:HALF, :], hxb[n]], axis=0)

    def prepare(n, carry):
        tail = hxa[n, HALF:, :].astype(F32)
        high, rest = tail[0:8, :], tail[8:16, :]
        place = lax.broadcasted_iota(jnp.int32, (8, A), 0)
        low = jnp.roll(rest, 4, axis=0)
        pos = high + jnp.where(place < 3, rest, 0.0) + jnp.where(place < 3, low, 0.0)
        p8[n] = pos
        pcol[at(n * A, A), :] = pos.T
        sender = dot(wst[...], features(n)).astype(BF).astype(F32)
        st[n] = sender.astype(BF)
        s_rows[at(n * A, A), :] = sender.T.astype(BF)
        ds[n] = jnp.zeros((C, A), F32)
        pg[n] = jnp.zeros((8, A), F32)
        return carry

    lax.fori_loop(0, NE, prepare, 0, unroll=8)
    place_targets(p8, relt, splt, refs)
    forward_pairs(count, pairs, pcol, diag, kern, sq, acc, st, lambda i: p8[i], NE + 2)
    kern[at((count + 1) * A, A), :] = jnp.zeros((A, K * A), BF)
    sq[at((count + 1) * A, A), :] = jnp.full((A, A), 25.0, F32)
    for b in range(NB):
        total = wr[:, 0:1] * acc[b, :, tile(0)]
        for k in range(1, K):
            total = total + wr[:, k : k + 1] * acc[b, :, tile(k)]
        wide[:, tile(b)] = total
    upd = dot(wut[...], wide[...].astype(BF))
    gain = upd * jax.nn.sigmoid(upd)
    for b in range(NB):
        wide[:, tile(b)] = features(target_index(b)).astype(F32) + gain[:, tile(b)]
    hidden = dot(wot[...], wide[...].astype(BF))
    dhid = silu_grad(hidden) * we[:, 0:1]
    for b in range(NB):
        real = (p8[target_index(b), 0:1, :] < FAR_TEST).astype(F32)
        wide[:, tile(b)] = dhid[:, tile(b)] * real
    dh2 = dot_wide(wo[...], wide[...]).astype(BF).astype(F32)
    dmsg = dot_wide(wu[...], dh2 * silu_grad(upd)).astype(BF).astype(F32)
    spread_weights(wr, dmsg, gt)
    wide[...] = dh2

    def senders(n):
        src, b, _ = decode(pairs[n])
        both = dot_nt(gt[b], kern[at(n * A, A), :])
        back = dot(ws[...], (both[0:C] + both[C:]).astype(BF))
        ds[src] = ds[src] + back.astype(BF).astype(F32)

    def squared_of(n):
        return lambda r: sq[at(n * A + r, ROWS), :]

    backward_pairs(
        count, pairs, p8, squared_of, (dker0, dker1), (slope0, slope1), s_rows, gt, pg, relt, splt, refs, tacc, senders
    )

    def finish(n, carry):
        outa_ref[n, 0:HALF, :] = ds[n, 0:HALF, :]
        outa_ref[n, HALF:, :] = pg[n]
        outb_ref[n] = ds[n, HALF:, :]
        return carry

    for b in range(NB):
        ds[target_index(b)] = ds[target_index(b)] + wide[:, tile(b)]

    lax.fori_loop(0, NE, finish, 0, unroll=8)


def first_backward(
    src_ref, xe, dha, dhb, upd_ref, embt, wst, wr, wu, pg,
    pcol, p8, diag, s_rows, gt, dker0, dker1, slope0, slope1, relt, splt, refs, tacc, wide, pairs,
):
    fill_diag(diag)
    count = live_pairs(src_ref, pairs)
    table = dot(wst[...], embt[...]).astype(BF)

    def prepare(n, carry):
        rows = xe[n]
        pcol[at(n * A, A), :] = rows.T
        p8[n] = marked(rows)
        sender = dot(table, species_onehot(rows[3:4, :]))
        s_rows[at(n * A, A), :] = sender.T.astype(BF)
        pg[n] = jnp.zeros((8, A), F32)
        return carry

    lax.fori_loop(0, NE, prepare, 0, unroll=8)
    place_targets(p8, relt, splt, refs)
    for b in range(NB):
        real = (p8[target_index(b), 0:1, :] < FAR_TEST).astype(F32)
        wide[0:HALF, tile(b)] = dha[b, 0:HALF, :].astype(BF).astype(F32) * real
        wide[HALF:, tile(b)] = dhb[b].astype(BF).astype(F32) * real
    dmsg = dot_wide(wu[...], wide[...] * silu_grad(upd_ref[...])).astype(BF).astype(F32)
    spread_weights(wr, dmsg, gt)

    def squared_of(n):
        src, b, kind = decode(pairs[n])
        rows = p8[target_index(b)]
        return lambda r: pair_squared(pcol, diag, src, kind, r, rows)

    backward_pairs(
        count, pairs, p8, squared_of, (dker0, dker1), (slope0, slope1), s_rows, gt, pg, relt, splt, refs, tacc,
        lambda n: None,
    )
    for b in range(NB):
        pg[target_index(b)] = pg[target_index(b)] + dha[b, HALF:, :]


SM = pl.BlockSpec(memory_space=pltpu.SMEM)
VM = pl.BlockSpec(memory_space=pltpu.VMEM)


def vm(*shape, kind=F32):
    return pltpu.VMEM(shape, kind)


PAIRS = pltpu.SMEM((NE + 4,), jnp.int32)


def params(mib):
    return pltpu.CompilerParams(vmem_limit_bytes=mib * 2**20)


def backward_scratch():
    return [vm(NB, 8, A), vm(NB, 16, A, kind=BF), vm(NB, 8, A), vm(NB, 8, A), vm(C, NB * A), PAIRS]


def call_first_forward(src, xe, *weights):
    return pl.pallas_call(
        first_forward,
        out_shape=(jax.ShapeDtypeStruct((NB, HALF + 16, A), BF), jax.ShapeDtypeStruct((NB, HALF, A), BF), jax.ShapeDtypeStruct((C, NB * A), F32)),
        in_specs=[SM] + [VM] * (1 + len(weights)),
        out_specs=(VM, VM, VM),
        scratch_shapes=[
            vm(NE * A, 8), vm(3 * A, A), vm(2 * A, K * A, kind=BF), vm(NB, 8, K * A), vm(NE, 8, A, kind=BF),
            vm(C, NB * A), PAIRS,
        ],
        compiler_params=params(20),
        name="first_forward",
    )(src, xe, *weights)


def call_second(src, hxa, hxb, *weights):
    return pl.pallas_call(
        second_both,
        out_shape=(jax.ShapeDtypeStruct((NE, HALF + 8, A), F32), jax.ShapeDtypeStruct((NE, HALF, A), F32)),
        in_specs=[SM] + [VM] * (2 + len(weights)),
        out_specs=(VM, VM),
        scratch_shapes=[
            vm(NE * A, 8), vm(NE, 8, A), vm(3 * A, A), vm((NE + 2) * A, K * A, kind=BF), vm((NE + 2) * A, A),
            vm(NB, C, K * A), vm(NE, C, A, kind=BF), vm(NE * A, C, kind=BF), vm(NB, 2 * C, K * A, kind=BF),
            vm(A, K * A, kind=BF), vm(A, K * A, kind=BF), vm(2 * A, A, kind=BF), vm(2 * A, A, kind=BF), vm(NE, C, A), vm(NE, 8, A),
        ] + backward_scratch(),
        compiler_params=params(54),
        name="second_both",
    )(src, hxa, hxb, *weights)


def call_first_backward(src, xe, dha, dhb, upd, *weights):
    return pl.pallas_call(
        first_backward,
        out_shape=jax.ShapeDtypeStruct((NE, 8, A), F32),
        in_specs=[SM] + [VM] * (4 + len(weights)),
        out_specs=VM,
        scratch_shapes=[
            vm(NE * A, 8), vm(NE, 8, A), vm(3 * A, A), vm(NE * A, C, kind=BF), vm(NB, 2 * C, K * A, kind=BF),
            vm(A, K * A, kind=BF), vm(A, K * A, kind=BF), vm(2 * A, A, kind=BF), vm(2 * A, A, kind=BF),
        ] + backward_scratch(),
        compiler_params=params(24),
        name="first_backward",
    )(src, xe, dha, dhb, upd, *weights)


def total_over_devices(value):
    count = lax.axis_size(AXES[0]) * lax.axis_size(AXES[1]) * lax.axis_size(AXES[2])
    rows = lax.all_to_all(jnp.broadcast_to(value, (count, 128)), AXES, 0, 0)
    return jnp.sum(rows[:, 0])


def local(
    positions, velocities, species, neighbour_blocks, embedding, w_send, w_radial, w_update, w_out, w_energy, masses
):
    kinds = embedding.shape[0]
    real = (species > 0)[..., None, :]
    inverse = 1.0 / masses[0]
    for s in range(1, kinds):
        inverse = jnp.where(species == s, 1.0 / masses[s], inverse)
    inverse = inverse[..., None, :]

    embt = jnp.pad(embedding.T, ((0, 0), (0, 8 - kinds)))
    wr = jnp.swapaxes(w_radial, 1, 2)
    wst = jnp.swapaxes(w_send, 1, 2)
    wut = jnp.swapaxes(w_update, 1, 2)
    we = w_energy[:, None]
    table = lax.reduce_precision(dot(wst[0], embt), 8, 7)
    wks = (wr[0][:, :, None] * table[:, None, :]).reshape(C, K * 8)

    lists = jnp.pad(neighbour_blocks.astype(F32), ((0, 0),) * 3 + ((0, A - 8),))[..., None, :]
    rest = jnp.concatenate(
        [species.astype(F32)[..., None, :], lists, jnp.zeros(species.shape[:3] + (3, A), F32)], axis=3
    )
    component = lax.broadcasted_iota(jnp.int32, positions.shape, 3)

    def placed(coords):
        away = jnp.where(real | (component > 0), coords, FAR)
        return halo_up(jnp.concatenate([away, rest], axis=3))

    own_src = slot_sources(neighbour_blocks, 0)

    def forces(ext, up_src):
        xe = ext.reshape(NE, 8, A)
        paya, payb, upd = call_first_forward(up_src, xe, embt, wks, wut[0])
        hxa = halo_down(paya.reshape(2, 2, 2, HALF + 16, A), (0, 1, 2)).reshape(NE, HALF + 16, A)
        hxb = halo_down(payb.reshape(2, 2, 2, HALF, A), (1, 2, 0)).reshape(NE, HALF, A)
        grada, gradb = call_second(
            own_src, hxa, hxb, w_send[1], wst[1], wr[1], w_update[1], wut[1], w_out, w_out.T, we
        )
        dha = fold_down(grada.reshape(4, 4, 4, HALF + 8, A), (2, 1, 0)).reshape(NB, HALF + 8, A)
        dhb = fold_down(gradb.reshape(4, 4, 4, HALF, A), (0, 2, 1)).reshape(NB, HALF, A)
        slopes = call_first_backward(up_src, xe, dha, dhb, upd, embt, wst[0], wr[0], w_update[0])
        return -fold_up(slopes.reshape(4, 4, 4, 8, A))[:, :, :, 0:3, :]

    ext = placed(positions)
    up_src = slot_sources(
        ext[1:3, 1:3, 1:3, 4, 0:8].astype(jnp.int32), 1
    )
    force_now = forces(ext, up_src)
    half_kick = velocities + 0.5 * time_step * force_now * inverse
    coords = positions + time_step * half_kick
    travelled = time_step * half_kick
    force_now = forces(placed(coords), up_src)
    velocity = half_kick + 0.5 * time_step * force_now * inverse
    local_kinetic = jnp.sum(real.astype(F32) * 0.5 / inverse * velocity * velocity)
    kinetic = total_over_devices(local_kinetic)
    slot_total = positions.size // 3 * lax.axis_size("gx") * lax.axis_size("gy") * lax.axis_size("gz")
    factor = jnp.sqrt(target_slot * slot_total / (kinetic + tiny_eps))
    return (travelled, velocity * factor)


def solution(mesh):
    spatial5 = P("gx", "gy", "gz", None, None)
    spatial4 = P("gx", "gy", "gz", None)
    return jax.shard_map(
        local,
        mesh=mesh,
        in_specs=(spatial5, spatial5, spatial4, spatial4) + (P(),) * 7,
        out_specs=(spatial5, spatial5),
        check_vma=False,
    )
```

```python
import math

import jax
import jax.numpy as jnp
from jax import lax
from jax.experimental import pallas as pl
from jax.experimental.pallas import tpu as pltpu
from jax.sharding import PartitionSpec as P

AXES = ("gx", "gy", "gz")
FAR = 1e12
FAR_TEST = 1e11
HUGE = 1e30
LOG2E = 1.4426950408889634
A = 128
C = 64
K = 8
NB = 8
NE = 64
ROWS = 32
HALF = 32
BF = jnp.bfloat16
F32 = jnp.float32
time_step = 1.0
target_slot = 0.25
tiny_eps = 1e-06


def ring(cells, axis, sign):
    count = lax.axis_size(axis)
    return lax.ppermute(cells, axis, [(i, (i + sign) % count) for i in range(count)])


def halo_up(cells):
    for dim, axis in enumerate(AXES):
        cells = jnp.concatenate([cells, ring(cells, axis, -1)], axis=dim)
    return cells


def halo_down(cells, order):
    for dim in order:
        cells = jnp.concatenate([ring(cells, AXES[dim], 1), cells], axis=dim)
    return cells


def fold_down(grid, order):
    for dim in order:
        low = lax.slice_in_dim(grid, 0, 2, axis=dim).astype(BF)
        grid = lax.slice_in_dim(grid, 2, 4, axis=dim) + ring(low, AXES[dim], -1).astype(F32)
    return grid


def fold_up(grid):
    for dim in (2, 1, 0):
        high = lax.slice_in_dim(grid, 2, 4, axis=dim)
        grid = lax.slice_in_dim(grid, 0, 2, axis=dim) + ring(high, AXES[dim], 1)
    return grid


def slot_sources(lists, shift):
    live = lists < 27
    offset = jnp.where(live, lists, 13)
    steps = (offset // 9 - 1, offset // 3 % 3 - 1, offset % 3 - 1)
    source = jnp.zeros_like(lists)
    for dim, axis in enumerate(AXES):
        total = 2 * lax.axis_size(axis)
        place = lax.broadcasted_iota(jnp.int32, lists.shape, dim)
        here = (2 * lax.axis_index(axis) + shift + place) % total + steps[dim]
        live = live & (here >= 0) & (here < total)
        source = source * 4 + place + 1 + steps[dim]
    return jnp.where(live, source, -1).reshape(NB, 8)


def dot(a, b):
    return lax.dot_general(a, b, (((1,), (0,)), ((), ())), preferred_element_type=F32)


def dot_nt(a, b):
    return lax.dot_general(a, b, (((1,), (1,)), ((), ())), preferred_element_type=F32)


def silu_grad(x):
    gate = jax.nn.sigmoid(x)
    return gate * (1.0 + x * (1.0 - gate))


def target_index(b):
    return ((b // 4 + 1) * 4 + (b // 2 % 2 + 1)) * 4 + b % 2 + 1


DEAD = 1024


def live_pairs(src_ref, pairs):
    count = jnp.int32(1)
    pairs[0] = DEAD
    for b in range(NB):
        for q in range(8):
            entry = src_ref[b, q]
            pairs[count] = entry + NE * b + jnp.where(entry == target_index(b), 0, 512)
            count = count + (entry >= 0).astype(jnp.int32)
    pairs[count] = DEAD
    pairs[count + 1] = DEAD
    return count - 1


def decode(code):
    return code % NE, code // NE % NB, code // 512


def fill_diag(diag):
    rows = lax.broadcasted_iota(jnp.int32, (A, A), 0)
    cols = lax.broadcasted_iota(jnp.int32, (A, A), 1)
    diag[0:A, :] = jnp.where(rows == cols, HUGE, 0.0)
    diag[A : 2 * A, :] = jnp.zeros((A, A), F32)
    diag[2 * A : 3 * A, :] = jnp.full((A, A), HUGE, F32)


def at(start, size):
    return pl.ds(pl.multiple_of(start, size), size)


def pair_squared(pcol, diag, src, kind, r, rows):
    cols = pcol[at(src * A + r, ROWS), :]
    dx = cols[:, 0:1] - rows[0:1, :]
    dy = cols[:, 1:2] - rows[1:2, :]
    dz = cols[:, 2:3] - rows[2:3, :]
    return jnp.minimum(dx * dx + dy * dy + dz * dz + diag[at(kind * A + r, ROWS), :], 25.0)


def pair_terms(squared):
    soft = squared + 0.25
    inv = lax.rsqrt(soft)
    u = soft * inv * 1.6 - 0.5
    t = 1.0 - squared * 0.04
    bell = jnp.exp2(u * u * (-LOG2E))
    growth = jnp.exp2(u * (2.0 * LOG2E))
    return inv, u, t, bell, growth


def store_kernel(pcol, diag, kern, sq, base, src, kind, rows):
    for r in range(0, A, ROWS):
        squared = pair_squared(pcol, diag, src, kind, r, rows)
        if sq is not None:
            sq[at(base + r, ROWS), :] = squared
        _, _, t, bell, growth = pair_terms(squared)
        value = bell * t * t
        for k in range(K):
            kern[at(base + r, ROWS), k * A : (k + 1) * A] = (value * math.exp(-k * k)).astype(BF)
            if k < K - 1:
                value = value * growth


def pair_slopes(squared_of, dker, slope):
    for r in range(0, A, ROWS):
        inv, u, t, bell, growth = pair_terms(squared_of(r))
        def weight(k):
            return dker[r : r + ROWS, tile(k)].astype(F32) * math.exp(-k * k)

        value = weight(K - 1)
        first = value
        for k in range(K - 2, 0, -1):
            value = value * growth + weight(k)
            first = first * growth + value
        first = first * growth
        value = value * growth + weight(0)
        out = (bell * t) * (value * (-0.08) + (t * inv * 1.6) * (first - u * value))
        high, low = halves(out)
        slope[r : r + ROWS, :] = high
        slope[A + r : A + r + ROWS, :] = low


def split16(rel):
    high = rel.astype(BF).astype(F32)
    return jnp.concatenate([high, rel - high], axis=0).astype(BF)


def halves(value):
    high = value.astype(BF)
    return high, (value - high.astype(F32)).astype(BF)


def dot_wide(weights, value):
    high, low = halves(value)
    return dot(weights, high) + dot(weights, low)


def moment_grad(rel, moments):
    total = moments[0:8, :] + moments[8:16, :]
    return 2.0 * (rel * total[3:4, :] - total)


def marked(rows):
    place = lax.broadcasted_iota(jnp.int32, (8, A), 0)
    return jnp.where(place == 3, 1.0, jnp.where(place < 3, rows, 0.0))


def species_onehot(row):
    return (lax.broadcasted_iota(jnp.int32, (8, A), 0).astype(F32) == row).astype(BF)


def reference_point(rows):
    place = lax.broadcasted_iota(jnp.int32, (8, A), 0)
    return jnp.where(place < 3, rows[:, 0:1], 0.0)


def tile(b):
    return slice(b * A, (b + 1) * A)


def forward_pairs(count, pairs, pcol, diag, kern, sq, acc, lhs, rows_of, slots):
    kern[0:A, :] = jnp.zeros((A, K * A), BF)
    acc[...] = jnp.zeros_like(acc)

    def multiply(n):
        src, b, _ = decode(pairs[n])
        acc[b] = acc[b] + dot(lhs[src], kern[at(n % slots * A, A), :])

    def step(n, carry):
        multiply(n - 1)
        src, b, kind = decode(pairs[n])
        store_kernel(pcol, diag, kern, sq, n % slots * A, src, kind, rows_of(target_index(b)))
        return carry

    lax.fori_loop(1, count + 1, step, 0)
    multiply(count)


def backward_pairs(
    count, pairs, p8, squared_of, dkers, slopes, s_rows, gt, pg, relt, splt, refs, tacc, extra
):
    tacc[...] = jnp.zeros_like(tacc)

    def slope_weights(n, dker):
        src, b, _ = decode(pairs[n])
        dker[...] = dot(jnp.concatenate([s_rows[at(src * A, A), :]] * 2, axis=1), gt[b]).astype(BF)

    def moments(n, slope):
        src, b, _ = decode(pairs[n])
        rel_s = p8[src] - refs[b]
        split_s = split16(rel_s)
        side_t = dot(jnp.concatenate([split_s, split_s], axis=1), slope[...])
        side_s = dot_nt(splt[b], slope[0:A, :]) + dot_nt(splt[b], slope[A:, :])
        pg[src] = pg[src] + moment_grad(rel_s, side_s)
        tacc[b] = tacc[b] + moment_grad(relt[b], side_t)

    slope_weights(1, dkers[0])

    def step(m, carry):
        n = 2 * m + 1
        slope_weights(n + 1, dkers[1])
        pair_slopes(squared_of(n), dkers[0], slopes[0])
        extra(n)
        slope_weights(n + 2, dkers[0])
        moments(n, slopes[0])
        pair_slopes(squared_of(n + 1), dkers[1], slopes[1])
        extra(n + 1)
        moments(n + 1, slopes[1])
        return carry

    lax.fori_loop(0, (count + 1) // 2, step, 0)
    for b in range(NB):
        pg[target_index(b)] = pg[target_index(b)] + tacc[b]


def spread_weights(wr, dmsg, gt):
    for b in range(NB):
        for k in range(K):
            high, low = halves(wr[:, k : k + 1] * dmsg[:, tile(b)])
            gt[b, 0:C, tile(k)] = high
            gt[b, C : 2 * C, tile(k)] = low


def place_targets(p8, relt, splt, refs):
    for b in range(NB):
        rows = p8[target_index(b)]
        refs[b] = reference_point(rows)
        relt[b] = rows - refs[b]
        splt[b] = split16(relt[b])


def first_forward(src_ref, xe, embt, wks, wut, paya_ref, payb_ref, upd_ref, pcol, diag, kern, acc, hot, cat, pairs):
    fill_diag(diag)
    count = live_pairs(src_ref, pairs)

    def prepare(n, carry):
        rows = xe[n]
        pcol[at(n * A, A), :] = rows.T
        hot[n] = species_onehot(rows[3:4, :])
        return carry

    lax.fori_loop(0, NE, prepare, 0, unroll=8)
    forward_pairs(count, pairs, pcol, diag, kern, None, acc, hot, lambda i: xe[i], 2)
    for b in range(NB):
        for k in range(K):
            cat[k * 8 : (k + 1) * 8, tile(b)] = acc[b, :, tile(k)]
    w_high, w_low = halves(wks[...])
    c_high, c_low = halves(cat[...])
    msg = dot(w_high, c_high) + (dot(w_high, c_low) + dot(w_low, c_high))
    upd = dot(wut[...], msg.astype(BF))
    upd_ref[...] = upd
    gain = upd * jax.nn.sigmoid(upd)
    for b in range(NB):
        rows = xe[target_index(b)]
        h0 = dot(embt[...], species_onehot(rows[3:4, :]))
        h1 = h0 + gain[:, tile(b)]
        paya_ref[b, 0:HALF, :] = h1[0:HALF].astype(BF)
        payb_ref[b] = h1[HALF:].astype(BF)
        pos = marked(rows)
        high = pos.astype(BF).astype(F32)
        mid = (pos - high).astype(BF).astype(F32)
        low = pos - high - mid
        place = lax.broadcasted_iota(jnp.int32, (8, A), 0)
        tail = jnp.where(place < 3, mid, 0.0) + jnp.where(place >= 4, jnp.roll(low, 4, axis=0), 0.0)
        paya_ref[b, HALF:, :] = jnp.concatenate([high, tail], axis=0).astype(BF)


def second_both(
    src_ref, hxa, hxb, ws, wst, wr, wu, wut, wo, wot, we, outa_ref, outb_ref,
    pcol, p8, diag, kern, sq, acc, st, s_rows, gt, dker0, dker1, slope0, slope1, ds, pg, relt, splt, refs, tacc, wide, pairs,
):
    fill_diag(diag)
    count = live_pairs(src_ref, pairs)

    def features(n):
        return jnp.concatenate([hxa[n, 0:HALF, :], hxb[n]], axis=0)

    def prepare(n, carry):
        tail = hxa[n, HALF:, :].astype(F32)
        high, rest = tail[0:8, :], tail[8:16, :]
        place = lax.broadcasted_iota(jnp.int32, (8, A), 0)
        low = jnp.roll(rest, 4, axis=0)
        pos = high + jnp.where(place < 3, rest, 0.0) + jnp.where(place < 3, low, 0.0)
        p8[n] = pos
        pcol[at(n * A, A), :] = pos.T
        sender = dot(wst[...], features(n)).astype(BF).astype(F32)
        st[n] = sender.astype(BF)
        s_rows[at(n * A, A), :] = sender.T.astype(BF)
        ds[n] = jnp.zeros((C, A), F32)
        pg[n] = jnp.zeros((8, A), F32)
        return carry

    lax.fori_loop(0, NE, prepare, 0, unroll=8)
    place_targets(p8, relt, splt, refs)
    forward_pairs(count, pairs, pcol, diag, kern, sq, acc, st, lambda i: p8[i], NE + 2)
    kern[at((count + 1) * A, A), :] = jnp.zeros((A, K * A), BF)
    sq[at((count + 1) * A, A), :] = jnp.full((A, A), 25.0, F32)
    for b in range(NB):
        total = wr[:, 0:1] * acc[b, :, tile(0)]
        for k in range(1, K):
            total = total + wr[:, k : k + 1] * acc[b, :, tile(k)]
        wide[:, tile(b)] = total
    upd = dot(wut[...], wide[...].astype(BF))
    gain = upd * jax.nn.sigmoid(upd)
    for b in range(NB):
        wide[:, tile(b)] = features(target_index(b)).astype(F32) + gain[:, tile(b)]
    hidden = dot(wot[...], wide[...].astype(BF))
    dhid = silu_grad(hidden) * we[:, 0:1]
    for b in range(NB):
        real = (p8[target_index(b), 0:1, :] < FAR_TEST).astype(F32)
        wide[:, tile(b)] = dhid[:, tile(b)] * real
    dh2 = dot_wide(wo[...], wide[...]).astype(BF).astype(F32)
    dmsg = dot_wide(wu[...], dh2 * silu_grad(upd)).astype(BF).astype(F32)
    spread_weights(wr, dmsg, gt)
    wide[...] = dh2

    def senders(n):
        src, b, _ = decode(pairs[n])
        both = dot_nt(gt[b], kern[at(n * A, A), :])
        back = dot(ws[...], (both[0:C] + both[C:]).astype(BF))
        ds[src] = ds[src] + back.astype(BF).astype(F32)

    def squared_of(n):
        return lambda r: sq[at(n * A + r, ROWS), :]

    backward_pairs(
        count, pairs, p8, squared_of, (dker0, dker1), (slope0, slope1), s_rows, gt, pg, relt, splt, refs, tacc, senders
    )

    def finish(n, carry):
        outa_ref[n, 0:HALF, :] = ds[n, 0:HALF, :]
        outa_ref[n, HALF:, :] = pg[n]
        outb_ref[n] = ds[n, HALF:, :]
        return carry

    for b in range(NB):
        ds[target_index(b)] = ds[target_index(b)] + wide[:, tile(b)]

    lax.fori_loop(0, NE, finish, 0, unroll=8)


def first_backward(
    src_ref, xe, dha, dhb, upd_ref, embt, wst, wr, wu, pg,
    pcol, p8, diag, s_rows, gt, dker0, dker1, slope0, slope1, relt, splt, refs, tacc, wide, pairs,
):
    fill_diag(diag)
    count = live_pairs(src_ref, pairs)
    table = dot(wst[...], embt[...]).astype(BF)

    def prepare(n, carry):
        rows = xe[n]
        pcol[at(n * A, A), :] = rows.T
        p8[n] = marked(rows)
        sender = dot(table, species_onehot(rows[3:4, :]))
        s_rows[at(n * A, A), :] = sender.T.astype(BF)
        pg[n] = jnp.zeros((8, A), F32)
        return carry

    lax.fori_loop(0, NE, prepare, 0, unroll=8)
    place_targets(p8, relt, splt, refs)
    for b in range(NB):
        real = (p8[target_index(b), 0:1, :] < FAR_TEST).astype(F32)
        wide[0:HALF, tile(b)] = dha[b, 0:HALF, :].astype(BF).astype(F32) * real
        wide[HALF:, tile(b)] = dhb[b].astype(BF).astype(F32) * real
    dmsg = dot_wide(wu[...], wide[...] * silu_grad(upd_ref[...])).astype(BF).astype(F32)
    spread_weights(wr, dmsg, gt)

    def squared_of(n):
        src, b, kind = decode(pairs[n])
        rows = p8[target_index(b)]
        return lambda r: pair_squared(pcol, diag, src, kind, r, rows)

    backward_pairs(
        count, pairs, p8, squared_of, (dker0, dker1), (slope0, slope1), s_rows, gt, pg, relt, splt, refs, tacc,
        lambda n: None,
    )
    for b in range(NB):
        pg[target_index(b)] = pg[target_index(b)] + dha[b, HALF:, :]


SM = pl.BlockSpec(memory_space=pltpu.SMEM)
VM = pl.BlockSpec(memory_space=pltpu.VMEM)


def vm(*shape, kind=F32):
    return pltpu.VMEM(shape, kind)


PAIRS = pltpu.SMEM((NE + 4,), jnp.int32)


def params(mib):
    return pltpu.CompilerParams(vmem_limit_bytes=mib * 2**20)


def backward_scratch():
    return [vm(NB, 8, A), vm(NB, 16, A, kind=BF), vm(NB, 8, A), vm(NB, 8, A), vm(C, NB * A), PAIRS]


def call_first_forward(src, xe, *weights):
    return pl.pallas_call(
        first_forward,
        out_shape=(jax.ShapeDtypeStruct((NB, HALF + 16, A), BF), jax.ShapeDtypeStruct((NB, HALF, A), BF), jax.ShapeDtypeStruct((C, NB * A), F32)),
        in_specs=[SM] + [VM] * (1 + len(weights)),
        out_specs=(VM, VM, VM),
        scratch_shapes=[
            vm(NE * A, 8), vm(3 * A, A), vm(2 * A, K * A, kind=BF), vm(NB, 8, K * A), vm(NE, 8, A, kind=BF),
            vm(C, NB * A), PAIRS,
        ],
        compiler_params=params(20),
        name="first_forward",
    )(src, xe, *weights)


def call_second(src, hxa, hxb, *weights):
    return pl.pallas_call(
        second_both,
        out_shape=(jax.ShapeDtypeStruct((NE, HALF + 8, A), F32), jax.ShapeDtypeStruct((NE, HALF, A), F32)),
        in_specs=[SM] + [VM] * (2 + len(weights)),
        out_specs=(VM, VM),
        scratch_shapes=[
            vm(NE * A, 8), vm(NE, 8, A), vm(3 * A, A), vm((NE + 2) * A, K * A, kind=BF), vm((NE + 2) * A, A),
            vm(NB, C, K * A), vm(NE, C, A, kind=BF), vm(NE * A, C, kind=BF), vm(NB, 2 * C, K * A, kind=BF),
            vm(A, K * A, kind=BF), vm(A, K * A, kind=BF), vm(2 * A, A, kind=BF), vm(2 * A, A, kind=BF), vm(NE, C, A), vm(NE, 8, A),
        ] + backward_scratch(),
        compiler_params=params(54),
        name="second_both",
    )(src, hxa, hxb, *weights)


def call_first_backward(src, xe, dha, dhb, upd, *weights):
    return pl.pallas_call(
        first_backward,
        out_shape=jax.ShapeDtypeStruct((NE, 8, A), F32),
        in_specs=[SM] + [VM] * (4 + len(weights)),
        out_specs=VM,
        scratch_shapes=[
            vm(NE * A, 8), vm(NE, 8, A), vm(3 * A, A), vm(NE * A, C, kind=BF), vm(NB, 2 * C, K * A, kind=BF),
            vm(A, K * A, kind=BF), vm(A, K * A, kind=BF), vm(2 * A, A, kind=BF), vm(2 * A, A, kind=BF),
        ] + backward_scratch(),
        compiler_params=params(24),
        name="first_backward",
    )(src, xe, dha, dhb, upd, *weights)


def total_over_devices(value):
    count = lax.axis_size(AXES[0]) * lax.axis_size(AXES[1]) * lax.axis_size(AXES[2])
    rows = lax.all_to_all(jnp.broadcast_to(value, (count, 128)), AXES, 0, 0)
    return jnp.sum(rows[:, 0])


def local(
    positions, velocities, species, neighbour_blocks, embedding, w_send, w_radial, w_update, w_out, w_energy, masses
):
    kinds = embedding.shape[0]
    real = (species > 0)[..., None, :]
    inverse = 1.0 / masses[0]
    for s in range(1, kinds):
        inverse = jnp.where(species == s, 1.0 / masses[s], inverse)
    inverse = inverse[..., None, :]

    embt = jnp.pad(embedding.T, ((0, 0), (0, 8 - kinds)))
    wr = jnp.swapaxes(w_radial, 1, 2)
    wst = jnp.swapaxes(w_send, 1, 2)
    wut = jnp.swapaxes(w_update, 1, 2)
    we = w_energy[:, None]
    table = lax.reduce_precision(dot(wst[0], embt), 8, 7)
    wks = (wr[0][:, :, None] * table[:, None, :]).reshape(C, K * 8)

    lists = jnp.pad(neighbour_blocks.astype(F32), ((0, 0),) * 3 + ((0, A - 8),))[..., None, :]
    rest = jnp.concatenate(
        [species.astype(F32)[..., None, :], lists, jnp.zeros(species.shape[:3] + (3, A), F32)], axis=3
    )
    component = lax.broadcasted_iota(jnp.int32, positions.shape, 3)

    def placed(coords, rest):
        away = jnp.where(real | (component > 0), coords, FAR)
        cells = halo_up(jnp.concatenate([away, rest], axis=3))
        return jnp.pad(cells, ((0, 0),) * 3 + ((0, 8 - cells.shape[3]), (0, 0)))

    own_src = slot_sources(neighbour_blocks, 0)

    def forces(ext, up_src):
        xe = ext.reshape(NE, 8, A)
        paya, payb, upd = call_first_forward(up_src, xe, embt, wks, wut[0])
        hxa = halo_down(paya.reshape(2, 2, 2, HALF + 16, A), (0, 1, 2)).reshape(NE, HALF + 16, A)
        hxb = halo_down(payb.reshape(2, 2, 2, HALF, A), (1, 2, 0)).reshape(NE, HALF, A)
        grada, gradb = call_second(
            own_src, hxa, hxb, w_send[1], wst[1], wr[1], w_update[1], wut[1], w_out, w_out.T, we
        )
        dha = fold_down(grada.reshape(4, 4, 4, HALF + 8, A), (2, 1, 0)).reshape(NB, HALF + 8, A)
        dhb = fold_down(gradb.reshape(4, 4, 4, HALF, A), (0, 2, 1)).reshape(NB, HALF, A)
        slopes = call_first_backward(up_src, xe, dha, dhb, upd, embt, wst[0], wr[0], w_update[0])
        return -fold_up(slopes.reshape(4, 4, 4, 8, A)[:, :, :, 0:4, :])[:, :, :, 0:3, :]

    ext = placed(positions, rest)
    up_src = slot_sources(
        ext[1:3, 1:3, 1:3, 4, 0:8].astype(jnp.int32), 1
    )
    force_now = forces(ext, up_src)
    half_kick = velocities + 0.5 * time_step * force_now * inverse
    coords = positions + time_step * half_kick
    travelled = time_step * half_kick
    force_now = forces(placed(coords, rest[:, :, :, 0:1, :]), up_src)
    velocity = half_kick + 0.5 * time_step * force_now * inverse
    local_kinetic = jnp.sum(real.astype(F32) * 0.5 / inverse * velocity * velocity)
    kinetic = total_over_devices(local_kinetic)
    slot_total = positions.size // 3 * lax.axis_size("gx") * lax.axis_size("gy") * lax.axis_size("gz")
    factor = jnp.sqrt(target_slot * slot_total / (kinetic + tiny_eps))
    return (travelled, velocity * factor)


def solution(mesh):
    spatial5 = P("gx", "gy", "gz", None, None)
    spatial4 = P("gx", "gy", "gz", None)
    return jax.shard_map(
        local,
        mesh=mesh,
        in_specs=(spatial5, spatial5, spatial4, spatial4) + (P(),) * 7,
        out_specs=(spatial5, spatial5),
        check_vma=False,
    )
```
